32 devices in a mesh: tile: 8 (over z, y), grp: 4 (over x, core).
Axes of the slice: x: 2, y: 2, z: 4, core: 2. Of those that a mesh axis runs over, the one named last changes fastest.
Arguments:
- soil_water: float32 [6, 2097152], P(None, ('tile', 'grp')), may hold values from 0.1 to 0.9
- rainfall: float32 [2097152], P(('tile', 'grp')), may hold values from 0.005 to 0.2
- drain_coef: float32 [6, 2097152], P(None, ('tile', 'grp')), may hold values from 0.02 to 0.5
- cell_storage: float32 [2097152], P(('tile', 'grp')), may hold values from 0.01 to 2
- release_rate: float32 [2097152], P(('tile', 'grp')), may hold values from 0.05 to 0.8
- downstream: int32 [2097152], P(('tile', 'grp')), may hold values from 1 to 128, as said below
- block_owner: int32 [16384, 1], P(('tile', 'grp')), may hold values from 0 to 31; in each aligned block of 512 rows (0 to 511, 512 to 1023, ...) at most 32 rows name the same one
- outlet_reach: int32 [16384], P(('tile', 'grp')), may hold values from 0 to 127
- river_storage: float32 [4, 1024], P('grp', 'tile'), may hold values from 0.02 to 0.5
- river_lag: float32 [4, 1024], P('grp', 'tile'), may hold values from 0 to 1
Outputs:
- soil_out: float32 [6, 2097152], P(None, ('tile', 'grp'))
- storage_out: float32 [2097152], P(('tile', 'grp'))
- section: float32 [4, 1024], P('grp', 'tile')
The draws below stay inside these ranges and needn't reach their ends.
Inputs may be any that keep to these rules, and one draw needn't show every extreme that they name: `downstream`: within its block of 128 cells a cell drains to a later cell of the block, or to 128, the block's outlet. `block_owner`: of the 512 blocks of one device, at most 32 have the same owner.
All inputs are finite; a program needn't handle non-finite values.
Results may differ from the reference program's by a relative error of at most 0.0003.
Values sent between devices are 32-bit elements; how exact they have to be, the bound alone decides.
A program may use at most 64 MiB of HBM per device.

```python
import math
import jax
import jax.numpy as jnp
import numpy as np
from jax import lax

SOIL = 6
CELL = 128
BLK_DEV = 512
REACH = 128
SUB = 4
CAP = 32
RIVERS = 4
RIVER_LEN = 1024
NBLOCKS = 16384
LAND = 2097152
DEVICES = 32


def draw_downstream(key, part):
    position = jnp.arange(LAND, dtype=jnp.int32) % CELL
    return jax.random.randint(key, (LAND,), position + 1, CELL + 1).astype(jnp.int32)


def draw_river_lag(key, part):
    stochastic_root_token, stochastic_placement_token, stochastic_downpour_token = jax.random.split(jax.random.fold_in(key, 7), 3)
    tensor_extents = (RIVERS, RIVER_LEN)
    spread = jnp.exp(jax.random.uniform(stochastic_root_token, tensor_extents, jnp.float32, jnp.log(0.2), jnp.log(2.0)))
    starting_integer_entropy = spread / RIVER_LEN
    spots = jax.random.randint(stochastic_placement_token, (RIVERS, 3), 0, RIVER_LEN)
    places = jnp.arange(RIVER_LEN, dtype=jnp.int32)
    deluged_grid_points = jnp.any(places[None, :, None] == spots[:, None, :], axis=2)
    sudden_downpour_episode = jax.random.uniform(stochastic_downpour_token, tensor_extents, jnp.float32, 0.25, 1.0)
    return jnp.where(deluged_grid_points, sudden_downpour_episode, starting_integer_entropy).astype(jnp.float32)


def set_ends(array, own_key, smallest, largest):
    place = [jax.random.randint(jax.random.fold_in(own_key, axis), (), 0, length) for axis, length in enumerate(array.shape)]
    widest = array.shape.index(max(array.shape))
    beside = place[:widest] + [(place[widest] + 1) % array.shape[widest]] + place[widest + 1:]
    return array.at[tuple(place)].set(smallest).at[tuple(beside)].set(largest)


def block_levels(rng, extent, cuts, least, high):
    def one(dim, shards_of):
        steps = jax.random.uniform(jax.random.fold_in(jax.random.fold_in(rng, 6), dim), (shards_of,), jnp.float32, least / len(cuts), high / len(cuts))
        return jnp.repeat(jnp.exp(steps), extent[dim] // shards_of).reshape((-1,) + (1,) * (len(extent) - dim - 1))

    level = one(*cuts[0])
    for cut in cuts[1:]:
        level = level * one(*cut)
    return level


def shared_out(stream_key, own, number, rows, number_of, top, reach, lean):
    order = jax.random.permutation(stream_key, number_of)
    crowded, usual = portions_of(number_of, rows * top, reach, lean, True), portions_of(number_of, rows * top, reach, lean, False)
    places = jnp.arange(number_of)

    def named(lengths, turn):
        used = int((lengths > 0).sum())
        fixed = max(1, used // 4)
        shifted = fixed + (places - fixed + turn * (used - fixed)) % max(1, number_of - fixed)
        return jnp.zeros((number_of,), jnp.int32).at[order[jnp.where(places < fixed, places, shifted)]].set(jnp.asarray(lengths, jnp.int32))

    lengths = jnp.where(number % 4 == 0, named(crowded, number // 4), named(usual, number - number // 4 - 1))
    mixed = jax.random.permutation(jax.random.fold_in(own, 3), number_of)
    donor, receiver = mixed[0:number_of // 2 * 2:2], mixed[1:number_of // 2 * 2:2]
    slack = jnp.minimum(lengths[donor] - 1, reach - lengths[receiver]) // 2
    slack = jnp.where((donor == order[0]) | (receiver == order[0]) | (lengths[receiver] == 0), 0, jnp.maximum(slack, 0))
    shifted = jax.random.randint(jax.random.fold_in(own, 4), (number_of // 2,), 0, 1 << 20) % (slack + 1)
    lengths = lengths.at[donor].add(-shifted).at[receiver].add(shifted)
    items = jnp.searchsorted(jnp.cumsum(lengths), jnp.arange(rows * top), side="right").astype(jnp.int32)
    grid = items.reshape(top, rows).T
    grid = grid[jax.random.permutation(jax.random.fold_in(own, 1), rows)]
    turn = jax.random.randint(jax.random.fold_in(own, 2), (rows, 1), 0, top)
    return jnp.take_along_axis(grid, (jnp.arange(top)[None, :] + turn) % top, axis=1)


def portions_of(count, total, reach, lean, full):
    loads = [(1 << 20) // math.isqrt(rank ** lean) + 1 for rank in range(1, count + 1)]
    largest = reach if full else min(reach, max(-(-total // count), total * loads[0] // sum(loads)))
    least = 1 if total - largest >= count - 1 else 0
    holding, spare = [largest] + [least] * (count - 1), total - largest - least * (count - 1)
    while spare > 0:
        free = [i for i in range(1, count) if holding[i] < largest] or [i for i in range(1, count) if holding[i] < reach]
        mass, remaining = sum([loads[i] for i in free]), spare
        for i in free:
            more = min(reach - holding[i], max(1, remaining * loads[i] // mass), spare)
            holding[i] = holding[i] + more
            spare = spare - more
    return np.array(holding)


def setup_inputs(seed: int = 0) -> dict:
    keys = jax.random.split(jax.random.key(seed), 11)
    soil_water = jnp.clip(0.1 + 0.79999997 * jax.random.uniform(keys[0], (SOIL, LAND), jnp.float32) ** block_levels(keys[0], (SOIL, LAND), ((1, 32),), -0.2, 0.2), 0.1, 0.9)
    rainfall = jnp.clip(jnp.exp(math.log(0.2) - 3.6888795 * jax.random.uniform(keys[1], (LAND,), jnp.float32) ** block_levels(keys[1], (LAND,), ((0, 32),), -0.2, 0.2)), 0.005, 0.2)
    drain_coef = jnp.clip(jnp.exp(math.log(0.5) - 3.218876 * jax.random.uniform(keys[2], (SOIL, LAND), jnp.float32) ** block_levels(keys[2], (SOIL, LAND), ((1, 32),), -0.2, 0.2)), 0.02, 0.5)
    cell_storage = jnp.clip(jnp.exp(math.log(2.0) - 5.2983174 * jax.random.uniform(keys[3], (LAND,), jnp.float32) ** block_levels(keys[3], (LAND,), ((0, 32),), -0.2, 0.2)), 0.01, 2.0)
    release_rate = jnp.clip(jnp.exp(math.log(0.8) - 2.7725887 * jax.random.uniform(keys[4], (LAND,), jnp.float32) ** block_levels(keys[4], (LAND,), ((0, 32),), -0.2, 0.2)), 0.05, 0.8)
    downstream = draw_downstream(jax.random.fold_in(keys[10], 71), 0)
    block_owner_keys = jax.random.split(jax.random.fold_in(keys[6], 1), NBLOCKS // BLK_DEV)
    block_owner_turns = jax.random.permutation(jax.random.fold_in(keys[6], 3), NBLOCKS // BLK_DEV)
    block_owner = jax.vmap(lambda own, number: shared_out(jax.random.fold_in(keys[6], 2), own, number, BLK_DEV, DEVICES, 1, CAP, 2))(block_owner_keys, block_owner_turns).reshape((NBLOCKS, 1))
    outlet_reach = set_ends(jax.random.randint(keys[7], (NBLOCKS,), 0, REACH), jax.random.fold_in(keys[7], 1), 0, REACH - 1).astype(jnp.int32)
    river_storage = jnp.clip(jnp.exp(math.log(0.5) - 3.218876 * jax.random.uniform(keys[8], (RIVERS, RIVER_LEN), jnp.float32) ** block_levels(keys[8], (RIVERS, RIVER_LEN), ((0, 4), (1, 8)), -0.2, 0.2)), 0.02, 0.5)
    river_lag = draw_river_lag(jax.random.fold_in(keys[10], 71), 0)
    return {"soil_water": soil_water, "rainfall": rainfall, "drain_coef": drain_coef, "cell_storage": cell_storage, "release_rate": release_rate, "downstream": downstream, "block_owner": block_owner, "outlet_reach": outlet_reach, "river_storage": river_storage, "river_lag": river_lag}


recharge_share = 0.2


def land_step(soil_water, rainfall, drain_coef):
    top_layer = soil_water[0]
    surface = rainfall * top_layer * top_layer
    soaked = rainfall - surface
    drained = drain_coef * soil_water * soil_water * soil_water
    inflow = jnp.concatenate([soaked[None], drained[:-1]], axis=0)
    return soil_water + inflow - drained, surface + drained[-1]


def route_turn(storage, share, release_rate, downstream, back):
    width = storage.shape[-1]
    targets = jnp.arange(width, dtype=jnp.int32)
    links = (downstream[:, :, None] == targets[None, None, :]).astype(jnp.float32)
    leaving = (downstream == width).astype(jnp.float32)
    factor = jnp.where(downstream == width, back[:, None], 1.0)
    release = release_rate * storage * factor
    upstream = jnp.einsum("gk,gki->gi", release, links, precision=lax.Precision.HIGHEST)
    outlet = jnp.sum(release * leaving, axis=1)
    return storage + share + upstream - release, outlet


def reference(soil_water, rainfall, drain_coef, cell_storage, release_rate, downstream, block_owner, outlet_reach, river_storage, river_lag):
    soil_mid, runoff = land_step(soil_water, rainfall, drain_coef)

    def blocked(values):
        return values.reshape(DEVICES, BLK_DEV, CELL)

    share = blocked(runoff / SUB)
    rates = blocked(release_rate)
    links = blocked(downstream)
    storage = blocked(cell_storage)
    owner = block_owner[:, 0].astype(jnp.int32)
    river_index = owner % RIVERS
    segment = owner // RIVERS
    position = (river_index * RIVER_LEN + segment * REACH + outlet_reach).astype(jnp.int32)
    weight = 1.0 / (1.0 + river_lag)
    volume = river_storage

    def advance(previous, column):
        flow_now = column[0] * previous + column[1]
        return flow_now, flow_now

    def route_device(parts):
        return route_turn(parts[0], parts[1], parts[2], parts[3], parts[4])

    flow = volume
    for turn in range(SUB):
        back = (1.0 / (1.0 + volume.reshape(-1)[position])).reshape(DEVICES, BLK_DEV)
        storage, outlets = lax.map(route_device, (storage, share, rates, links, back))
        lateral = jax.ops.segment_sum(outlets.reshape(-1), position, num_segments=RIVERS * RIVER_LEN) / CELL
        feed = weight * (volume + lateral.reshape(RIVERS, RIVER_LEN))
        _, flows = lax.scan(advance, jnp.zeros((RIVERS,), jnp.float32), (weight.T, feed.T))
        flow = flows.T
        volume = river_lag * flow
    section = jnp.log1p(flow)
    storage_out = storage.reshape(-1)
    flooded = storage_out / (storage_out + 1.0)
    soil_out = soil_mid.at[0].add(recharge_share * flooded * (1.0 - soil_mid[0]))
    return soil_out, storage_out, section
```

```python
import functools
import math

import jax
import jax.numpy as jnp
from jax import lax
from jax.experimental import pallas as pl
from jax.experimental.pallas import tpu as pltpu
from jax.sharding import PartitionSpec as P

SUB = 4
MOMENTS = SUB * (SUB + 1) // 2
MESH = pl.DeviceIdType.MESH

recharge_share = 0.2


def split(x):
    high = x.astype(jnp.bfloat16)
    low = (x - high.astype(jnp.float32)).astype(jnp.bfloat16)
    return high, low


def lanes_of(shape):
    return lax.broadcasted_iota(jnp.int32, shape, len(shape) - 1)


def pick(values, index):
    return jnp.take_along_axis(values, index, axis=1)


def sort_rows(key, lane):
    width = key.shape[1]
    size = 2
    while size <= width:
        step = size // 2
        while step:
            other = pick(key, lane ^ step)
            low = ((lane & step) != 0) == ((lane & size) != 0)
            key = jnp.where(low, jnp.minimum(key, other), jnp.maximum(key, other))
            step //= 2
        size *= 2
    return key


def route_kernel(
    share_ref, storage_ref, rate_ref, down_ref, owner_ref, reach_ref, up_ref, agg_ref, moment_ref
):
    step = pl.program_id(0)
    rows, width = share_ref.shape
    devices, _, reaches = agg_ref.shape
    blocks = owner_ref.shape[1]
    lane = lanes_of((rows, width))
    down = down_ref[...]
    key = sort_rows((down * width + lane).astype(jnp.float32), lane).astype(jnp.int32)
    order = key % width
    target = key // width
    ends = jnp.zeros_like(lane)
    hop = width // 2
    while hop:
        ends = jnp.where(pick(target, ends + (hop - 1)) <= lane, ends + hop, ends)
        hop //= 2
    square = (width, width)
    before = (lax.broadcasted_iota(jnp.int32, square, 0) < lanes_of(square)).astype(jnp.bfloat16)
    share = share_ref[...]
    rate = rate_ref[...]
    storage = storage_ref[...]
    leaving = jnp.where(down == width, rate, 0.0)
    powers = [leaving]
    for _ in range(SUB - 1):
        powers.append(powers[-1] * leaving)
    sums = jnp.zeros((rows, width), jnp.float32)
    column = 0
    for power in powers:
        value = jnp.sum(power * storage, axis=1, keepdims=True)
        sums = jnp.where(lane == column, value, sums)
        column += 1
    for turn in range(SUB):
        release = rate * storage
        high, low = split(pick(release, order))
        running = jnp.dot(high, before, preferred_element_type=jnp.float32) + jnp.dot(
            low, before, preferred_element_type=jnp.float32
        )
        upto = pick(running, ends)
        upstream = jnp.where(lane == 0, 0.0, upto - pltpu.roll(upto, 1, 1))
        gained = share + upstream
        up_ref[turn] = gained
        storage = storage + gained - release
        for power in powers[: SUB - 1 - turn]:
            value = jnp.sum(power * gained, axis=1, keepdims=True)
            sums = jnp.where(lane == column, value, sums)
            column += 1
    moment_ref[pl.ds(pl.multiple_of(step * rows, rows), rows), :] = sums

    @pl.when(step == pl.num_programs(0) - 1)
    def _():
        flat = moment_ref[...].T[:16]
        mine = lax.broadcasted_iota(jnp.int32, (devices, blocks), 0) == owner_ref[...]
        mine = mine.astype(jnp.float32)[:, None, :]
        hits = lax.broadcasted_iota(jnp.int32, (reaches, blocks), 0) == reach_ref[...]
        hits = hits.astype(jnp.float32).astype(jnp.bfloat16)
        total = jnp.zeros((devices * 16, reaches), jnp.float32)
        for part in split(flat):
            spread = (mine * part.astype(jnp.float32)[None]).reshape(devices * 16, blocks)
            total = total + lax.dot_general(
                spread.astype(jnp.bfloat16),
                hits,
                (((1,), (1,)), ((), ())),
                preferred_element_type=jnp.float32,
            )
        agg_ref[...] = total.reshape(devices, 16, reaches)[:, :MOMENTS, :]


def exchange_kernel(
    groups,
    devices,
    agg_ref,
    volume_ref,
    lag_ref,
    out_ref,
    landed,
    mine,
    send_sem,
    recv_sem,
    send_all,
    recv_all,
):
    me = lax.axis_index("tile") * groups + lax.axis_index("grp")

    def peer_at(step):
        peer = lax.rem(me + step, devices)
        return peer, (peer // groups, lax.rem(peer, groups))

    barrier = pltpu.get_barrier_semaphore()

    def greet(step, carry):
        pl.semaphore_signal(barrier, inc=1, device_id=peer_at(step)[1], device_id_type=MESH)
        return carry

    lax.fori_loop(1, devices, greet, 0)
    pl.semaphore_wait(barrier, devices - 1)

    def part(step):
        peer, place = peer_at(step)
        return pltpu.make_async_remote_copy(
            src_ref=agg_ref.at[peer],
            dst_ref=landed.at[step],
            send_sem=send_sem.at[step],
            recv_sem=recv_sem.at[step],
            device_id=place,
            device_id_type=MESH,
        )

    def whole(step):
        return pltpu.make_async_remote_copy(
            src_ref=mine,
            dst_ref=out_ref.at[me],
            send_sem=send_all.at[step],
            recv_sem=recv_all.at[step],
            device_id=peer_at(step)[1],
            device_id_type=MESH,
        )

    def start(copy):
        def body(step, carry):
            copy(step).start()
            return carry

        lax.fori_loop(1, devices, body, 0)

    def finish(copy):
        def body(step, carry):
            copy(step).wait()
            return carry

        lax.fori_loop(1, devices, body, 0)

    start(part)
    landed[0] = agg_ref[me]
    finish(part)
    mine[pl.ds(0, MOMENTS), :] = jnp.sum(landed[...], axis=0)
    mine[pl.ds(MOMENTS, 1), :] = volume_ref[...]
    mine[pl.ds(MOMENTS + 1, 1), :] = lag_ref[...]
    start(whole)
    out_ref[me] = mine[...]
    finish(whole)


def simulate(groups, river, width):
    devices, reaches = river[0].shape
    shape = (devices, reaches)
    lane = lanes_of(shape)
    row = lax.broadcasted_iota(jnp.int32, shape, 0)
    volume, lag = river[MOMENTS], river[MOMENTS + 1]
    weight = 1.0 / (1.0 + lag)
    held = list(river[:SUB])
    gained, at = [], SUB
    for turn in range(SUB - 1):
        gained.append(river[at : at + SUB - 1 - turn])
        at += SUB - 1 - turn

    def ladder(gain, place, axis, first, size):
        steps, step = [], first
        while step < size:
            inside = place >= step
            steps.append((step, jnp.where(inside, gain, 0.0)))
            gain = jnp.where(inside, gain * pltpu.roll(gain, step, axis), gain)
            step *= 2
        return steps, gain

    def climb(steps, value, axis):
        for step, gain in steps:
            value = value + gain * pltpu.roll(value, step, axis)
        return value

    def last(value):
        return jnp.broadcast_to(value[:, reaches - 1 :], shape)

    within, gain = ladder(weight, lane, 1, 1, reaches)
    across, _ = ladder(last(gain), row, 0, groups, devices)
    backs, flow = [], volume
    for turn in range(SUB):
        back = 1.0 / (1.0 + volume)
        backs.append(back)
        feed = weight * (volume + back * held[0] / width)
        offset = climb(within, feed, 1)
        head = climb(across, last(offset), 0)
        if devices > groups:
            head = jnp.where(row >= groups, pltpu.roll(head, groups, 0), 0.0)
        else:
            head = jnp.zeros_like(head)
        flow = gain * head + offset
        volume = lag * flow
        if turn < SUB - 1:
            held = [
                held[j] + gained[turn][j] - back * held[j + 1] for j in range(SUB - 1 - turn)
            ]
    return backs, flow


def settle_kernel(
    groups,
    river_ref,
    storage_ref,
    rate_ref,
    down_ref,
    owner_ref,
    reach_ref,
    up_ref,
    storage_out_ref,
    section_ref,
    table_ref,
    place_ref,
):
    step = pl.program_id(0)
    rows, width = storage_ref.shape
    devices, _, reaches = river_ref.shape
    blocks = owner_ref.shape[1]

    @pl.when(step == 0)
    def _():
        river = [river_ref[:, m, :] for m in range(MOMENTS + 2)]
        backs, flow = simulate(groups, river, width)
        me = lax.axis_index("tile") * groups + lax.axis_index("grp")
        own = lax.broadcasted_iota(jnp.int32, flow.shape, 0) == me
        section_ref[...] = jnp.log1p(jnp.sum(jnp.where(own, flow, 0.0), axis=0, keepdims=True))
        for turn in range(SUB):
            high, low = split(backs[turn])
            table_ref[0, :, turn * reaches : (turn + 1) * reaches] = high
            table_ref[1, :, turn * reaches : (turn + 1) * reaches] = low
        both = jnp.concatenate(
            [
                jnp.broadcast_to(owner_ref[...].astype(jnp.float32), (8, blocks)),
                jnp.broadcast_to(reach_ref[...].astype(jnp.float32), (8, blocks)),
                jnp.zeros((112, blocks), jnp.float32),
            ],
            axis=0,
        )
        place_ref[...] = both.T

    place = place_ref[pl.ds(pl.multiple_of(step * rows, rows), rows), :].astype(jnp.int32)
    owner, reach = place[:, 0:1], place[:, 8:9]
    mine = (lanes_of((rows, devices)) == owner).astype(jnp.float32).astype(jnp.bfloat16)
    found = jnp.dot(mine, table_ref[0], preferred_element_type=jnp.float32) + jnp.dot(
        mine, table_ref[1], preferred_element_type=jnp.float32
    )
    hit = lanes_of((rows, reaches)) == reach
    leaving = down_ref[...] == width
    rate = rate_ref[...]
    storage = storage_ref[...]
    for turn in range(SUB):
        back = jnp.sum(
            jnp.where(hit, found[:, turn * reaches : (turn + 1) * reaches], 0.0),
            axis=1,
            keepdims=True,
        )
        release = rate * storage * jnp.where(leaving, back, 1.0)
        storage = storage + up_ref[turn] - release
    storage_out_ref[...] = storage


def land_step(soil_water, rainfall, drain_coef):
    top_layer = soil_water[0]
    surface = rainfall * top_layer * top_layer
    soaked = rainfall - surface
    drained = drain_coef * soil_water * soil_water * soil_water
    inflow = jnp.concatenate([soaked[None], drained[:-1]], axis=0)
    return (soil_water + inflow - drained, surface + drained[-1])


def local(
    soil_water,
    rainfall,
    drain_coef,
    cell_storage,
    release_rate,
    downstream,
    block_owner,
    outlet_reach,
    river_storage,
    river_lag,
):
    groups = lax.axis_size("grp")
    devices = lax.axis_size("tile") * groups
    blocks = block_owner.shape[0]
    width = rainfall.shape[0] // blocks
    reaches = river_storage.shape[1]
    rows = math.gcd(blocks, 64)
    soil_mid, runoff = land_step(soil_water, rainfall, drain_coef)
    share = (runoff / SUB).reshape(blocks, width)
    storage = cell_storage.reshape(blocks, width)
    rate = release_rate.reshape(blocks, width)
    down = downstream.reshape(blocks, width)
    owner = block_owner.reshape(1, blocks)
    reach = outlet_reach.reshape(1, blocks)

    tile = pl.BlockSpec((rows, width), lambda i: (i, 0))
    line = pl.BlockSpec((1, blocks), lambda i: (0, 0))
    stack = pl.BlockSpec((SUB, rows, width), lambda i: (0, i, 0))
    gained, agg = pl.pallas_call(
        route_kernel,
        grid=(blocks // rows,),
        out_shape=(
            jax.ShapeDtypeStruct((SUB, blocks, width), jnp.float32),
            jax.ShapeDtypeStruct((devices, MOMENTS, reaches), jnp.float32),
        ),
        in_specs=[tile, tile, tile, tile, line, line],
        out_specs=(stack, pl.BlockSpec((devices, MOMENTS, reaches), lambda i: (0, 0, 0))),
        scratch_shapes=[pltpu.VMEM((blocks, width), jnp.float32)],
        compiler_params=pltpu.CompilerParams(vmem_limit_bytes=40 * 1024 * 1024),
    )(share, storage, rate, down, owner, reach)

    vmem = pl.BlockSpec(memory_space=pltpu.VMEM)
    river = pl.pallas_call(
        functools.partial(exchange_kernel, groups, devices),
        out_shape=jax.ShapeDtypeStruct((devices, MOMENTS + 2, reaches), jnp.float32),
        in_specs=[vmem] * 3,
        out_specs=vmem,
        scratch_shapes=[
            pltpu.VMEM((devices, MOMENTS, reaches), jnp.float32),
            pltpu.VMEM((MOMENTS + 2, reaches), jnp.float32),
            pltpu.SemaphoreType.DMA((devices,)),
            pltpu.SemaphoreType.DMA((devices,)),
            pltpu.SemaphoreType.DMA((devices,)),
            pltpu.SemaphoreType.DMA((devices,)),
        ],
        compiler_params=pltpu.CompilerParams(
            collective_id=0, has_side_effects=True, vmem_limit_bytes=40 * 1024 * 1024
        ),
    )(agg, river_storage, river_lag)

    storage_out, section = pl.pallas_call(
        functools.partial(settle_kernel, groups),
        grid=(blocks // rows,),
        out_shape=(
            jax.ShapeDtypeStruct((blocks, width), jnp.float32),
            jax.ShapeDtypeStruct((1, reaches), jnp.float32),
        ),
        in_specs=[
            pl.BlockSpec((devices, MOMENTS + 2, reaches), lambda i: (0, 0, 0)),
            tile,
            tile,
            tile,
            line,
            line,
            stack,
        ],
        out_specs=(tile, pl.BlockSpec((1, reaches), lambda i: (0, 0))),
        scratch_shapes=[
            pltpu.VMEM((2, devices, SUB * reaches), jnp.bfloat16),
            pltpu.VMEM((blocks, 128), jnp.float32),
        ],
        compiler_params=pltpu.CompilerParams(vmem_limit_bytes=40 * 1024 * 1024),
    )(river, storage, rate, down, owner, reach, gained)

    storage_out = storage_out.reshape(-1)
    flooded = storage_out / (storage_out + 1.0)
    soil_out = soil_mid.at[0].add(recharge_share * flooded * (1.0 - soil_mid[0]))
    return (soil_out, storage_out, section)


def solution(mesh):
    placed = (
        P(None, ("tile", "grp")),
        P(("tile", "grp")),
        P(None, ("tile", "grp")),
        P(("tile", "grp")),
        P(("tile", "grp")),
        P(("tile", "grp")),
        P(("tile", "grp"), None),
        P(("tile", "grp")),
        P("grp", "tile"),
        P("grp", "tile"),
    )
    return jax.shard_map(
        local,
        mesh=mesh,
        in_specs=placed,
        out_specs=(P(None, ("tile", "grp")), P(("tile", "grp")), P("grp", "tile")),
        check_vma=False,
    )
```

```python
import functools
import math

import jax
import jax.numpy as jnp
from jax import lax
from jax.experimental import pallas as pl
from jax.experimental.pallas import tpu as pltpu
from jax.sharding import PartitionSpec as P

SUB = 4
MOMENTS = SUB * (SUB + 1) // 2
MESH = pl.DeviceIdType.MESH

recharge_share = 0.2


def split(x):
    high = x.astype(jnp.bfloat16)
    low = (x - high.astype(jnp.float32)).astype(jnp.bfloat16)
    return high, low


def lanes_of(shape):
    return lax.broadcasted_iota(jnp.int32, shape, len(shape) - 1)


def ones_where(mask):
    return mask.astype(jnp.float32).astype(jnp.bfloat16)


def pick(values, index):
    return jnp.take_along_axis(values, index, axis=1)


def sort_rows(key):
    width = key.shape[1]
    count = width // 8
    flipped = key.T
    parts = [flipped[v * 8 : v * 8 + 8] for v in range(count)]
    line = lax.broadcasted_iota(jnp.int32, parts[0].shape, 0)
    size = 2
    while size <= width:
        step = size // 2
        while step:
            after = list(parts)
            if step < count:
                for v in range(count):
                    if v & step:
                        continue
                    small = jnp.minimum(parts[v], parts[v | step])
                    large = jnp.maximum(parts[v], parts[v | step])
                    if size < count:
                        falling = bool(v & size)
                        after[v], after[v | step] = (large, small) if falling else (small, large)
                    elif size == width:
                        after[v], after[v | step] = small, large
                    else:
                        falling = (line & (size // count)) != 0
                        after[v] = jnp.where(falling, large, small)
                        after[v | step] = jnp.where(falling, small, large)
            else:
                hop = step // count
                upper = (line & hop) != 0
                low = jnp.logical_xor(upper, (line & (size // count)) == 0)
                for v in range(count):
                    here = parts[v]
                    other = jnp.where(upper, pltpu.roll(here, hop, 0), pltpu.roll(here, 8 - hop, 0))
                    after[v] = jnp.where(low, jnp.minimum(here, other), jnp.maximum(here, other))
            parts = after
            step //= 2
        size *= 2
    rows = jnp.concatenate(parts, axis=0).T
    lane = lanes_of(rows.shape)
    return pick(rows, (lane % count) * 8 + lane // count)


def route_kernel(
    share_ref, storage_ref, rate_ref, down_ref, owner_ref, reach_ref, up_ref, agg_ref, moment_ref
):
    step = pl.program_id(0)
    rows, width = share_ref.shape
    devices, _, reaches = agg_ref.shape
    blocks = owner_ref.shape[1]
    lane = lanes_of((rows, width))
    down = down_ref[...]
    key = sort_rows((down * width + lane).astype(jnp.float32)).astype(jnp.int32)
    order = key % width
    target = key // width
    ends = jnp.zeros_like(lane)
    hop = width // 2
    while hop:
        ends = jnp.where(pick(target, ends + (hop - 1)) <= lane, ends + hop, ends)
        hop //= 2
    square = (width, width)
    first, second = lax.broadcasted_iota(jnp.int32, square, 0), lanes_of(square)
    before = ones_where(first < second)

    def product(value, ones):
        return jnp.dot(
            jnp.concatenate(split(value), axis=1),
            jnp.concatenate([ones, ones], axis=0),
            preferred_element_type=jnp.float32,
        )

    share = share_ref[...]
    rate = rate_ref[...]
    storage = storage_ref[...]
    leaving = jnp.where(down == width, rate, 0.0)
    powers = [leaving]
    for _ in range(SUB - 1):
        powers.append(powers[-1] * leaving)
    sums = jnp.zeros((rows, width), jnp.float32)
    column = 0
    for power in powers:
        sums = sums + product(power * storage, ones_where(second == column))
        column += 1
    for turn in range(SUB):
        release = rate * storage
        upto = pick(product(pick(release, order), before), ends)
        upstream = jnp.where(lane == 0, 0.0, upto - pltpu.roll(upto, 1, 1))
        gained = share + upstream
        up_ref[turn] = gained
        storage = storage + gained - release
        for power in powers[: SUB - 1 - turn]:
            sums = sums + product(power * gained, ones_where(second == column))
            column += 1
    moment_ref[pl.ds(pl.multiple_of(step * rows, rows), rows), :] = sums

    @pl.when(step == pl.num_programs(0) - 1)
    def _():
        flat = moment_ref[...].T[:16]
        mine = lax.broadcasted_iota(jnp.int32, (devices, blocks), 0) == owner_ref[...]
        mine = mine.astype(jnp.float32)[:, None, :]
        hits = lax.broadcasted_iota(jnp.int32, (reaches, blocks), 0) == reach_ref[...]
        hits = hits.astype(jnp.float32).astype(jnp.bfloat16)
        total = jnp.zeros((devices * 16, reaches), jnp.float32)
        for part in split(flat):
            spread = (mine * part.astype(jnp.float32)[None]).reshape(devices * 16, blocks)
            total = total + lax.dot_general(
                spread.astype(jnp.bfloat16),
                hits,
                (((1,), (1,)), ((), ())),
                preferred_element_type=jnp.float32,
            )
        agg_ref[...] = total.reshape(devices, 16, reaches)[:, :MOMENTS, :]


def land_step(soil_water, rainfall, drain_coef):
    top_layer = soil_water[:1]
    soaked = rainfall - rainfall * top_layer * top_layer
    drained = drain_coef * soil_water * soil_water * soil_water
    inflow = jnp.concatenate([soaked, drained[:-1]], axis=0)
    return soil_water + inflow - drained


def exchange_kernel(
    groups,
    devices,
    agg_ref,
    volume_ref,
    lag_ref,
    soil_ref,
    coef_ref,
    rain_ref,
    out_ref,
    mid_ref,
    landed,
    mine,
    send_sem,
    recv_sem,
    send_all,
    recv_all,
):
    me = lax.axis_index("tile") * groups + lax.axis_index("grp")

    def peer_at(step):
        peer = lax.rem(me + step, devices)
        return peer, (peer // groups, lax.rem(peer, groups))

    barrier = pltpu.get_barrier_semaphore()

    def greet(step, carry):
        pl.semaphore_signal(barrier, inc=1, device_id=peer_at(step)[1], device_id_type=MESH)
        return carry

    lax.fori_loop(1, devices, greet, 0)
    pl.semaphore_wait(barrier, devices - 1)

    def part(step):
        peer, place = peer_at(step)
        return pltpu.make_async_remote_copy(
            src_ref=agg_ref.at[peer],
            dst_ref=landed.at[step],
            send_sem=send_sem.at[step],
            recv_sem=recv_sem.at[step],
            device_id=place,
            device_id_type=MESH,
        )

    def whole(step):
        return pltpu.make_async_remote_copy(
            src_ref=mine,
            dst_ref=out_ref.at[me],
            send_sem=send_all.at[step],
            recv_sem=recv_all.at[step],
            device_id=peer_at(step)[1],
            device_id_type=MESH,
        )

    def start(copy):
        def body(step, carry):
            copy(step).start()
            return carry

        lax.fori_loop(1, devices, body, 0)

    def finish(copy):
        def body(step, carry):
            copy(step).wait()
            return carry

        lax.fori_loop(1, devices, body, 0)

    start(part)
    landed[0] = agg_ref[me]
    span = math.gcd(soil_ref.shape[1], 2048)

    def land(turn, carry):
        at = pl.ds(pl.multiple_of(turn * span, span), span)
        mid_ref[:, at] = land_step(soil_ref[:, at], rain_ref[:, at], coef_ref[:, at])
        return carry

    lax.fori_loop(0, soil_ref.shape[1] // span, land, 0)
    finish(part)
    mine[pl.ds(0, MOMENTS), :] = jnp.sum(landed[...], axis=0)
    mine[pl.ds(MOMENTS, 1), :] = volume_ref[...]
    mine[pl.ds(MOMENTS + 1, 1), :] = lag_ref[...]
    start(whole)
    out_ref[me] = mine[...]
    finish(whole)


def simulate(groups, river, width):
    devices, reaches = river[0].shape
    shape = (devices, reaches)
    lane = lanes_of(shape)
    row = lax.broadcasted_iota(jnp.int32, shape, 0)
    volume, lag = river[MOMENTS], river[MOMENTS + 1]
    weight = 1.0 / (1.0 + lag)
    held = list(river[:SUB])
    gained, at = [], SUB
    for turn in range(SUB - 1):
        gained.append(river[at : at + SUB - 1 - turn])
        at += SUB - 1 - turn

    def ladder(gain, place, axis, first, size):
        steps, step = [], first
        while step < size:
            inside = place >= step
            steps.append((step, jnp.where(inside, gain, 0.0)))
            gain = jnp.where(inside, gain * pltpu.roll(gain, step, axis), gain)
            step *= 2
        return steps, gain

    def climb(steps, value, axis):
        for step, gain in steps:
            value = value + gain * pltpu.roll(value, step, axis)
        return value

    def last(value):
        return jnp.broadcast_to(value[:, reaches - 1 :], shape)

    within, gain = ladder(weight, lane, 1, 1, reaches)
    across, _ = ladder(last(gain), row, 0, groups, devices)
    backs, flow = [], volume
    for turn in range(SUB):
        back = 1.0 / (1.0 + volume)
        backs.append(back)
        feed = weight * (volume + back * held[0] / width)
        offset = climb(within, feed, 1)
        head = climb(across, last(offset), 0)
        if devices > groups:
            head = jnp.where(row >= groups, pltpu.roll(head, groups, 0), 0.0)
        else:
            head = jnp.zeros_like(head)
        flow = gain * head + offset
        volume = lag * flow
        if turn < SUB - 1:
            held = [
                held[j] + gained[turn][j] - back * held[j + 1] for j in range(SUB - 1 - turn)
            ]
    return backs, flow


def settle_kernel(
    groups,
    river_ref,
    storage_ref,
    rate_ref,
    down_ref,
    owner_ref,
    reach_ref,
    up_ref,
    storage_out_ref,
    section_ref,
    table_ref,
    place_ref,
):
    step = pl.program_id(0)
    rows, width = storage_ref.shape
    devices, _, reaches = river_ref.shape
    blocks = owner_ref.shape[1]

    @pl.when(step == 0)
    def _():
        river = [river_ref[:, m, :] for m in range(MOMENTS + 2)]
        backs, flow = simulate(groups, river, width)
        me = lax.axis_index("tile") * groups + lax.axis_index("grp")
        own = lax.broadcasted_iota(jnp.int32, flow.shape, 0) == me
        section_ref[...] = jnp.log1p(jnp.sum(jnp.where(own, flow, 0.0), axis=0, keepdims=True))
        for turn in range(SUB):
            high, low = split(backs[turn])
            table_ref[0, :, turn * reaches : (turn + 1) * reaches] = high
            table_ref[1, :, turn * reaches : (turn + 1) * reaches] = low
        both = jnp.concatenate(
            [
                jnp.broadcast_to(owner_ref[...].astype(jnp.float32), (8, blocks)),
                jnp.broadcast_to(reach_ref[...].astype(jnp.float32), (8, blocks)),
                jnp.zeros((112, blocks), jnp.float32),
            ],
            axis=0,
        )
        place_ref[...] = both.T

    place = place_ref[pl.ds(pl.multiple_of(step * rows, rows), rows), :].astype(jnp.int32)
    owner, reach = place[:, 0:1], place[:, 8:9]
    mine = (lanes_of((rows, devices)) == owner).astype(jnp.float32).astype(jnp.bfloat16)
    found = jnp.dot(mine, table_ref[0], preferred_element_type=jnp.float32) + jnp.dot(
        mine, table_ref[1], preferred_element_type=jnp.float32
    )
    hit = lanes_of((rows, reaches)) == reach
    leaving = down_ref[...] == width
    rate = rate_ref[...]
    storage = storage_ref[...]
    for turn in range(SUB):
        back = jnp.sum(
            jnp.where(hit, found[:, turn * reaches : (turn + 1) * reaches], 0.0),
            axis=1,
            keepdims=True,
        )
        release = rate * storage * jnp.where(leaving, back, 1.0)
        storage = storage + up_ref[turn] - release
    storage_out_ref[...] = storage


def local(
    soil_water,
    rainfall,
    drain_coef,
    cell_storage,
    release_rate,
    downstream,
    block_owner,
    outlet_reach,
    river_storage,
    river_lag,
):
    groups = lax.axis_size("grp")
    devices = lax.axis_size("tile") * groups
    blocks = block_owner.shape[0]
    width = rainfall.shape[0] // blocks
    reaches = river_storage.shape[1]
    rows = math.gcd(blocks, 128)
    top, deep = soil_water[0], soil_water[-1]
    runoff = rainfall * top * top + drain_coef[-1] * deep * deep * deep
    share = (runoff / SUB).reshape(blocks, width)
    storage = cell_storage.reshape(blocks, width)
    rate = release_rate.reshape(blocks, width)
    down = downstream.reshape(blocks, width)
    owner = block_owner.reshape(1, blocks)
    reach = outlet_reach.reshape(1, blocks)

    tile = pl.BlockSpec((rows, width), lambda i: (i, 0))
    line = pl.BlockSpec((1, blocks), lambda i: (0, 0))
    stack = pl.BlockSpec((SUB, rows, width), lambda i: (0, i, 0))
    gained, agg = pl.pallas_call(
        route_kernel,
        grid=(blocks // rows,),
        out_shape=(
            jax.ShapeDtypeStruct((SUB, blocks, width), jnp.float32),
            jax.ShapeDtypeStruct((devices, MOMENTS, reaches), jnp.float32),
        ),
        in_specs=[tile, tile, tile, tile, line, line],
        out_specs=(stack, pl.BlockSpec((devices, MOMENTS, reaches), lambda i: (0, 0, 0))),
        scratch_shapes=[pltpu.VMEM((blocks, width), jnp.float32)],
        compiler_params=pltpu.CompilerParams(vmem_limit_bytes=40 * 1024 * 1024),
    )(share, storage, rate, down, owner, reach)

    vmem = pl.BlockSpec(memory_space=pltpu.VMEM)
    river, soil_mid = pl.pallas_call(
        functools.partial(exchange_kernel, groups, devices),
        out_shape=(
            jax.ShapeDtypeStruct((devices, MOMENTS + 2, reaches), jnp.float32),
            jax.ShapeDtypeStruct(soil_water.shape, jnp.float32),
        ),
        in_specs=[vmem] * 6,
        out_specs=(vmem, vmem),
        scratch_shapes=[
            pltpu.VMEM((devices, MOMENTS, reaches), jnp.float32),
            pltpu.VMEM((MOMENTS + 2, reaches), jnp.float32),
            pltpu.SemaphoreType.DMA((devices,)),
            pltpu.SemaphoreType.DMA((devices,)),
            pltpu.SemaphoreType.DMA((devices,)),
            pltpu.SemaphoreType.DMA((devices,)),
        ],
        compiler_params=pltpu.CompilerParams(
            collective_id=0, has_side_effects=True, vmem_limit_bytes=40 * 1024 * 1024
        ),
    )(agg, river_storage, river_lag, soil_water, drain_coef, rainfall[None])

    storage_out, section = pl.pallas_call(
        functools.partial(settle_kernel, groups),
        grid=(blocks // rows,),
        out_shape=(
            jax.ShapeDtypeStruct((blocks, width), jnp.float32),
            jax.ShapeDtypeStruct((1, reaches), jnp.float32),
        ),
        in_specs=[
            pl.BlockSpec((devices, MOMENTS + 2, reaches), lambda i: (0, 0, 0)),
            tile,
            tile,
            tile,
            line,
            line,
            stack,
        ],
        out_specs=(tile, pl.BlockSpec((1, reaches), lambda i: (0, 0))),
        scratch_shapes=[
            pltpu.VMEM((2, devices, SUB * reaches), jnp.bfloat16),
            pltpu.VMEM((blocks, 128), jnp.float32),
        ],
        compiler_params=pltpu.CompilerParams(vmem_limit_bytes=40 * 1024 * 1024),
    )(river, storage, rate, down, owner, reach, gained)

    storage_out = storage_out.reshape(-1)
    flooded = storage_out / (storage_out + 1.0)
    layer = lax.broadcasted_iota(jnp.int32, soil_mid.shape, 0)
    wetter = recharge_share * flooded[None] * (1.0 - soil_mid)
    soil_out = jnp.where(layer == 0, soil_mid + wetter, soil_mid)
    return (soil_out, storage_out, section)


def solution(mesh):
    placed = (
        P(None, ("tile", "grp")),
        P(("tile", "grp")),
        P(None, ("tile", "grp")),
        P(("tile", "grp")),
        P(("tile", "grp")),
        P(("tile", "grp")),
        P(("tile", "grp"), None),
        P(("tile", "grp")),
        P("grp", "tile"),
        P("grp", "tile"),
    )
    return jax.shard_map(
        local,
        mesh=mesh,
        in_specs=placed,
        out_specs=(P(None, ("tile", "grp")), P(("tile", "grp")), P("grp", "tile")),
        check_vma=False,
    )
```

```python
import functools
import math

import jax
import jax.numpy as jnp
from jax import lax
from jax.experimental import pallas as pl
from jax.experimental.pallas import tpu as pltpu
from jax.sharding import PartitionSpec as P

SUB = 4
MOMENTS = SUB * (SUB + 1) // 2
MESH = pl.DeviceIdType.MESH

recharge_share = 0.2


def split(x):
    high = x.astype(jnp.bfloat16)
    low = (x - high.astype(jnp.float32)).astype(jnp.bfloat16)
    return high, low


def lanes_of(shape):
    return lax.broadcasted_iota(jnp.int32, shape, len(shape) - 1)


def ones_where(mask):
    return mask.astype(jnp.float32).astype(jnp.bfloat16)


def pick(values, index):
    return jnp.take_along_axis(values, index, axis=1)


def sort_rows(key):
    width = key.shape[1]
    count = width // 8
    flipped = key.T
    parts = [flipped[v * 8 : v * 8 + 8] for v in range(count)]
    line = lax.broadcasted_iota(jnp.int32, parts[0].shape, 0)
    size = 2
    while size <= width:
        step = size // 2
        while step:
            after = list(parts)
            if step < count:
                for v in range(count):
                    if v & step:
                        continue
                    small = jnp.minimum(parts[v], parts[v | step])
                    large = jnp.maximum(parts[v], parts[v | step])
                    if size < count:
                        falling = bool(v & size)
                        after[v], after[v | step] = (large, small) if falling else (small, large)
                    elif size == width:
                        after[v], after[v | step] = small, large
                    else:
                        falling = (line & (size // count)) != 0
                        after[v] = jnp.where(falling, large, small)
                        after[v | step] = jnp.where(falling, small, large)
            else:
                hop = step // count
                upper = (line & hop) != 0
                low = jnp.logical_xor(upper, (line & (size // count)) == 0)
                for v in range(count):
                    here = parts[v]
                    other = jnp.where(upper, pltpu.roll(here, hop, 0), pltpu.roll(here, 8 - hop, 0))
                    after[v] = jnp.where(low, jnp.minimum(here, other), jnp.maximum(here, other))
            parts = after
            step //= 2
        size *= 2
    rows = jnp.concatenate(parts, axis=0).T
    lane = lanes_of(rows.shape)
    return pick(rows, (lane % count) * 8 + lane // count)


def route_kernel(
    soil_ref,
    coef_ref,
    rain_ref,
    storage_ref,
    rate_ref,
    down_ref,
    owner_ref,
    reach_ref,
    up_ref,
    agg_ref,
    moment_ref,
    top_ref,
    deep_ref,
    drain_ref,
):
    step = pl.program_id(0)
    rows, width = storage_ref.shape
    devices, _, reaches = agg_ref.shape
    blocks = owner_ref.shape[1]
    lane = lanes_of((rows, width))
    down = down_ref[...]
    key = sort_rows((down * width + lane).astype(jnp.float32)).astype(jnp.int32)
    order = key % width
    target = key // width
    ends = jnp.zeros_like(lane)
    hop = width // 2
    while hop:
        ends = jnp.where(pick(target, ends + (hop - 1)) <= lane, ends + hop, ends)
        hop //= 2
    square = (width, width)
    first, second = lax.broadcasted_iota(jnp.int32, square, 0), lanes_of(square)
    before = ones_where(first < second)

    def product(value, ones):
        return jnp.dot(
            jnp.concatenate(split(value), axis=1),
            jnp.concatenate([ones, ones], axis=0),
            preferred_element_type=jnp.float32,
        )

    final = soil_ref.shape[0] - 1
    for b in range(rows):
        at = slice(b * width, (b + 1) * width)
        top_ref[b : b + 1, :] = soil_ref[0:1, at]
        deep_ref[b : b + 1, :] = soil_ref[final : final + 1, at]
        drain_ref[b : b + 1, :] = coef_ref[final : final + 1, at]
    top, deep = top_ref[...], deep_ref[...]
    runoff = rain_ref[...] * top * top + drain_ref[...] * deep * deep * deep
    share = runoff / SUB
    rate = rate_ref[...]
    storage = storage_ref[...]
    leaving = jnp.where(down == width, rate, 0.0)
    powers = [leaving]
    for _ in range(SUB - 1):
        powers.append(powers[-1] * leaving)
    sums = jnp.zeros((rows, width), jnp.float32)
    column = 0
    for power in powers:
        sums = sums + product(power * storage, ones_where(second == column))
        column += 1
    for turn in range(SUB):
        release = rate * storage
        upto = pick(product(pick(release, order), before), ends)
        upstream = jnp.where(lane == 0, 0.0, upto - pltpu.roll(upto, 1, 1))
        gained = share + upstream
        up_ref[turn] = gained
        storage = storage + gained - release
        for power in powers[: SUB - 1 - turn]:
            sums = sums + product(power * gained, ones_where(second == column))
            column += 1
    moment_ref[pl.ds(pl.multiple_of(step * rows, rows), rows), :] = sums

    @pl.when(step == pl.num_programs(0) - 1)
    def _():
        flat = moment_ref[...].T[:16]
        mine = lax.broadcasted_iota(jnp.int32, (devices, blocks), 0) == owner_ref[...]
        mine = mine.astype(jnp.float32)[:, None, :]
        hits = lax.broadcasted_iota(jnp.int32, (reaches, blocks), 0) == reach_ref[...]
        hits = hits.astype(jnp.float32).astype(jnp.bfloat16)
        total = jnp.zeros((devices * 16, reaches), jnp.float32)
        for part in split(flat):
            spread = (mine * part.astype(jnp.float32)[None]).reshape(devices * 16, blocks)
            total = total + lax.dot_general(
                spread.astype(jnp.bfloat16),
                hits,
                (((1,), (1,)), ((), ())),
                preferred_element_type=jnp.float32,
            )
        agg_ref[...] = total.reshape(devices, 16, reaches)[:, :MOMENTS, :]


def land_step(soil_water, rainfall, drain_coef):
    top_layer = soil_water[:1]
    soaked = rainfall - rainfall * top_layer * top_layer
    drained = drain_coef * soil_water * soil_water * soil_water
    inflow = jnp.concatenate([soaked, drained[:-1]], axis=0)
    return soil_water + inflow - drained


def exchange_kernel(
    groups,
    devices,
    agg_ref,
    volume_ref,
    lag_ref,
    soil_hbm,
    coef_hbm,
    rain_hbm,
    out_ref,
    mid_ref,
    soil_ref,
    coef_ref,
    rain_ref,
    load_sem,
    landed,
    mine,
    send_sem,
    recv_sem,
    send_all,
    recv_all,
):
    me = lax.axis_index("tile") * groups + lax.axis_index("grp")

    def peer_at(step):
        peer = lax.rem(me + step, devices)
        return peer, (peer // groups, lax.rem(peer, groups))

    loads = [
        pltpu.make_async_copy(soil_hbm, soil_ref, load_sem.at[0]),
        pltpu.make_async_copy(coef_hbm, coef_ref, load_sem.at[1]),
        pltpu.make_async_copy(rain_hbm, rain_ref, load_sem.at[2]),
    ]
    for load in loads:
        load.start()
    barrier = pltpu.get_barrier_semaphore()

    def greet(step, carry):
        pl.semaphore_signal(barrier, inc=1, device_id=peer_at(step)[1], device_id_type=MESH)
        return carry

    lax.fori_loop(1, devices, greet, 0)
    pl.semaphore_wait(barrier, devices - 1)

    def part(step):
        peer, place = peer_at(step)
        return pltpu.make_async_remote_copy(
            src_ref=agg_ref.at[peer],
            dst_ref=landed.at[step],
            send_sem=send_sem.at[step],
            recv_sem=recv_sem.at[step],
            device_id=place,
            device_id_type=MESH,
        )

    def whole(step):
        return pltpu.make_async_remote_copy(
            src_ref=mine,
            dst_ref=out_ref.at[me],
            send_sem=send_all.at[step],
            recv_sem=recv_all.at[step],
            device_id=peer_at(step)[1],
            device_id_type=MESH,
        )

    def start(copy):
        def body(step, carry):
            copy(step).start()
            return carry

        lax.fori_loop(1, devices, body, 0)

    def finish(copy):
        def body(step, carry):
            copy(step).wait()
            return carry

        lax.fori_loop(1, devices, body, 0)

    start(part)
    landed[0] = agg_ref[me]
    span = math.gcd(soil_ref.shape[1], 2048)

    def land(turn, carry):
        at = pl.ds(pl.multiple_of(turn * span, span), span)
        mid_ref[:, at] = land_step(soil_ref[:, at], rain_ref[:, at], coef_ref[:, at])
        return carry

    for load in loads:
        load.wait()
    lax.fori_loop(0, soil_ref.shape[1] // span, land, 0)
    finish(part)
    mine[pl.ds(0, MOMENTS), :] = jnp.sum(landed[...], axis=0)
    mine[pl.ds(MOMENTS, 1), :] = volume_ref[...]
    mine[pl.ds(MOMENTS + 1, 1), :] = lag_ref[...]
    start(whole)
    out_ref[me] = mine[...]
    finish(whole)


def simulate(groups, river, width):
    devices, reaches = river[0].shape
    shape = (devices, reaches)
    lane = lanes_of(shape)
    row = lax.broadcasted_iota(jnp.int32, shape, 0)
    volume, lag = river[MOMENTS], river[MOMENTS + 1]
    weight = 1.0 / (1.0 + lag)
    held = list(river[:SUB])
    gained, at = [], SUB
    for turn in range(SUB - 1):
        gained.append(river[at : at + SUB - 1 - turn])
        at += SUB - 1 - turn

    def ladder(gain, place, axis, first, size):
        steps, step = [], first
        while step < size:
            inside = place >= step
            steps.append((step, jnp.where(inside, gain, 0.0)))
            gain = jnp.where(inside, gain * pltpu.roll(gain, step, axis), gain)
            step *= 2
        return steps, gain

    def climb(steps, value, axis):
        for step, gain in steps:
            value = value + gain * pltpu.roll(value, step, axis)
        return value

    def last(value):
        return jnp.broadcast_to(value[:, reaches - 1 :], shape)

    within, gain = ladder(weight, lane, 1, 1, reaches)
    across, _ = ladder(last(gain), row, 0, groups, devices)
    backs, flow = [], volume
    for turn in range(SUB):
        back = 1.0 / (1.0 + volume)
        backs.append(back)
        feed = weight * (volume + back * held[0] / width)
        offset = climb(within, feed, 1)
        head = climb(across, last(offset), 0)
        if devices > groups:
            head = jnp.where(row >= groups, pltpu.roll(head, groups, 0), 0.0)
        else:
            head = jnp.zeros_like(head)
        flow = gain * head + offset
        volume = lag * flow
        if turn < SUB - 1:
            held = [
                held[j] + gained[turn][j] - back * held[j + 1] for j in range(SUB - 1 - turn)
            ]
    return backs, flow


def settle_kernel(
    groups,
    river_ref,
    storage_ref,
    rate_ref,
    down_ref,
    owner_ref,
    reach_ref,
    up_ref,
    mid_ref,
    storage_out_ref,
    section_ref,
    soil_out_ref,
    table_ref,
    place_ref,
    wet_ref,
):
    step = pl.program_id(0)
    rows, width = storage_ref.shape
    devices, _, reaches = river_ref.shape
    blocks = owner_ref.shape[1]

    @pl.when(step == 0)
    def _():
        river = [river_ref[:, m, :] for m in range(MOMENTS + 2)]
        backs, flow = simulate(groups, river, width)
        me = lax.axis_index("tile") * groups + lax.axis_index("grp")
        own = lax.broadcasted_iota(jnp.int32, flow.shape, 0) == me
        section_ref[...] = jnp.log1p(jnp.sum(jnp.where(own, flow, 0.0), axis=0, keepdims=True))
        for turn in range(SUB):
            high, low = split(backs[turn])
            table_ref[0, :, turn * reaches : (turn + 1) * reaches] = high
            table_ref[1, :, turn * reaches : (turn + 1) * reaches] = low
        both = jnp.concatenate(
            [
                jnp.broadcast_to(owner_ref[...].astype(jnp.float32), (8, blocks)),
                jnp.broadcast_to(reach_ref[...].astype(jnp.float32), (8, blocks)),
                jnp.zeros((112, blocks), jnp.float32),
            ],
            axis=0,
        )
        place_ref[...] = both.T

    place = place_ref[pl.ds(pl.multiple_of(step * rows, rows), rows), :].astype(jnp.int32)
    owner, reach = place[:, 0:1], place[:, 8:9]
    mine = (lanes_of((rows, devices)) == owner).astype(jnp.float32).astype(jnp.bfloat16)
    found = jnp.dot(mine, table_ref[0], preferred_element_type=jnp.float32) + jnp.dot(
        mine, table_ref[1], preferred_element_type=jnp.float32
    )
    hit = lanes_of((rows, reaches)) == reach
    leaving = down_ref[...] == width
    rate = rate_ref[...]
    storage = storage_ref[...]
    for turn in range(SUB):
        back = jnp.sum(
            jnp.where(hit, found[:, turn * reaches : (turn + 1) * reaches], 0.0),
            axis=1,
            keepdims=True,
        )
        release = rate * storage * jnp.where(leaving, back, 1.0)
        storage = storage + up_ref[turn] - release
    storage_out_ref[...] = storage
    wet_ref[...] = recharge_share * (storage / (storage + 1.0))
    soil_out_ref[1:, :] = mid_ref[1:, :]
    for b in range(rows):
        at = slice(b * width, (b + 1) * width)
        top = mid_ref[0:1, at]
        soil_out_ref[0:1, at] = top + wet_ref[b : b + 1, :] * (1.0 - top)


def local(
    soil_water,
    rainfall,
    drain_coef,
    cell_storage,
    release_rate,
    downstream,
    block_owner,
    outlet_reach,
    river_storage,
    river_lag,
):
    groups = lax.axis_size("grp")
    devices = lax.axis_size("tile") * groups
    blocks = block_owner.shape[0]
    width = rainfall.shape[0] // blocks
    reaches = river_storage.shape[1]
    rows = math.gcd(blocks, 128)
    rain = rainfall.reshape(blocks, width)
    storage = cell_storage.reshape(blocks, width)
    rate = release_rate.reshape(blocks, width)
    down = downstream.reshape(blocks, width)
    owner = block_owner.reshape(1, blocks)
    reach = outlet_reach.reshape(1, blocks)

    tile = pl.BlockSpec((rows, width), lambda i: (i, 0))
    layers = soil_water.shape[0]
    slab = pl.BlockSpec((layers, rows * width), lambda i: (0, i))
    line = pl.BlockSpec((1, blocks), lambda i: (0, 0))
    stack = pl.BlockSpec((SUB, rows, width), lambda i: (0, i, 0))
    gained, agg = pl.pallas_call(
        route_kernel,
        grid=(blocks // rows,),
        out_shape=(
            jax.ShapeDtypeStruct((SUB, blocks, width), jnp.float32),
            jax.ShapeDtypeStruct((devices, MOMENTS, reaches), jnp.float32),
        ),
        in_specs=[slab, slab, tile, tile, tile, tile, line, line],
        out_specs=(stack, pl.BlockSpec((devices, MOMENTS, reaches), lambda i: (0, 0, 0))),
        scratch_shapes=[pltpu.VMEM((blocks, width), jnp.float32)]
        + [pltpu.VMEM((rows, width), jnp.float32)] * 3,
        compiler_params=pltpu.CompilerParams(vmem_limit_bytes=40 * 1024 * 1024),
    )(soil_water, drain_coef, rain, storage, rate, down, owner, reach)

    vmem = pl.BlockSpec(memory_space=pltpu.VMEM)
    river, soil_mid = pl.pallas_call(
        functools.partial(exchange_kernel, groups, devices),
        out_shape=(
            jax.ShapeDtypeStruct((devices, MOMENTS + 2, reaches), jnp.float32),
            jax.ShapeDtypeStruct(soil_water.shape, jnp.float32),
        ),
        in_specs=[vmem] * 3 + [pl.BlockSpec(memory_space=pl.ANY)] * 3,
        out_specs=(vmem, vmem),
        scratch_shapes=[
            pltpu.VMEM(soil_water.shape, jnp.float32),
            pltpu.VMEM(soil_water.shape, jnp.float32),
            pltpu.VMEM((1, soil_water.shape[1]), jnp.float32),
            pltpu.SemaphoreType.DMA((3,)),
            pltpu.VMEM((devices, MOMENTS, reaches), jnp.float32),
            pltpu.VMEM((MOMENTS + 2, reaches), jnp.float32),
            pltpu.SemaphoreType.DMA((devices,)),
            pltpu.SemaphoreType.DMA((devices,)),
            pltpu.SemaphoreType.DMA((devices,)),
            pltpu.SemaphoreType.DMA((devices,)),
        ],
        compiler_params=pltpu.CompilerParams(
            collective_id=0, has_side_effects=True, vmem_limit_bytes=40 * 1024 * 1024
        ),
    )(agg, river_storage, river_lag, soil_water, drain_coef, rainfall[None])

    storage_out, section, soil_out = pl.pallas_call(
        functools.partial(settle_kernel, groups),
        grid=(blocks // rows,),
        out_shape=(
            jax.ShapeDtypeStruct((blocks, width), jnp.float32),
            jax.ShapeDtypeStruct((1, reaches), jnp.float32),
            jax.ShapeDtypeStruct(soil_water.shape, jnp.float32),
        ),
        in_specs=[
            pl.BlockSpec((devices, MOMENTS + 2, reaches), lambda i: (0, 0, 0)),
            tile,
            tile,
            tile,
            line,
            line,
            stack,
            slab,
        ],
        out_specs=(tile, pl.BlockSpec((1, reaches), lambda i: (0, 0)), slab),
        scratch_shapes=[
            pltpu.VMEM((2, devices, SUB * reaches), jnp.bfloat16),
            pltpu.VMEM((blocks, 128), jnp.float32),
            pltpu.VMEM((rows, width), jnp.float32),
        ],
        compiler_params=pltpu.CompilerParams(vmem_limit_bytes=40 * 1024 * 1024),
    )(river, storage, rate, down, owner, reach, gained, soil_mid)

    return (soil_out, storage_out.reshape(-1), section)


def solution(mesh):
    placed = (
        P(None, ("tile", "grp")),
        P(("tile", "grp")),
        P(None, ("tile", "grp")),
        P(("tile", "grp")),
        P(("tile", "grp")),
        P(("tile", "grp")),
        P(("tile", "grp"), None),
        P(("tile", "grp")),
        P("grp", "tile"),
        P("grp", "tile"),
    )
    return jax.shard_map(
        local,
        mesh=mesh,
        in_specs=placed,
        out_specs=(P(None, ("tile", "grp")), P(("tile", "grp")), P("grp", "tile")),
        check_vma=False,
    )
```

```python
import functools
import math

import jax
import jax.numpy as jnp
from jax import lax
from jax.experimental import pallas as pl
from jax.experimental.pallas import tpu as pltpu
from jax.sharding import PartitionSpec as P

SUB = 4
MOMENTS = SUB * (SUB + 1) // 2
MESH = pl.DeviceIdType.MESH

recharge_share = 0.2


def split(x):
    high = x.astype(jnp.bfloat16)
    low = (x - high.astype(jnp.float32)).astype(jnp.bfloat16)
    return high, low


def lanes_of(shape):
    return lax.broadcasted_iota(jnp.int32, shape, len(shape) - 1)


def ones_where(mask):
    return mask.astype(jnp.float32).astype(jnp.bfloat16)


def pick(values, index):
    return jnp.take_along_axis(values, index, axis=1)


def sort_rows(key):
    width = key.shape[1]
    count = width // 8
    flipped = key.T
    parts = [flipped[v * 8 : v * 8 + 8] for v in range(count)]
    line = lax.broadcasted_iota(jnp.int32, parts[0].shape, 0)
    size = 2
    while size <= width:
        step = size // 2
        while step:
            after = list(parts)
            if step < count:
                for v in range(count):
                    if v & step:
                        continue
                    small = jnp.minimum(parts[v], parts[v | step])
                    large = jnp.maximum(parts[v], parts[v | step])
                    if size < count:
                        falling = bool(v & size)
                        after[v], after[v | step] = (large, small) if falling else (small, large)
                    elif size == width:
                        after[v], after[v | step] = small, large
                    else:
                        falling = (line & (size // count)) != 0
                        after[v] = jnp.where(falling, large, small)
                        after[v | step] = jnp.where(falling, small, large)
            else:
                hop = step // count
                upper = (line & hop) != 0
                low = jnp.logical_xor(upper, (line & (size // count)) == 0)
                for v in range(count):
                    here = parts[v]
                    other = jnp.where(upper, pltpu.roll(here, hop, 0), pltpu.roll(here, 8 - hop, 0))
                    after[v] = jnp.where(low, jnp.minimum(here, other), jnp.maximum(here, other))
            parts = after
            step //= 2
        size *= 2
    rows = jnp.concatenate(parts, axis=0).T
    lane = lanes_of(rows.shape)
    return pick(rows, (lane % count) * 8 + lane // count)


def route_kernel(
    soil_ref,
    coef_ref,
    rain_ref,
    storage_ref,
    rate_ref,
    down_ref,
    owner_ref,
    reach_ref,
    up_ref,
    agg_ref,
    moment_ref,
    top_ref,
    deep_ref,
    drain_ref,
):
    step = pl.program_id(0)
    rows, width = storage_ref.shape
    devices, _, reaches = agg_ref.shape
    blocks = owner_ref.shape[1]
    lane = lanes_of((rows, width))
    down = down_ref[...]
    key = sort_rows((down * width + lane).astype(jnp.float32)).astype(jnp.int32)
    order = key % width
    target = key // width
    ends = jnp.zeros_like(lane)
    hop = width // 2
    while hop:
        ends = jnp.where(pick(target, ends + (hop - 1)) <= lane, ends + hop, ends)
        hop //= 2
    square = (width, width)
    first, second = lax.broadcasted_iota(jnp.int32, square, 0), lanes_of(square)
    before = ones_where(first < second)

    def product(value, ones):
        return jnp.dot(
            jnp.concatenate(split(value), axis=1),
            jnp.concatenate([ones, ones], axis=0),
            preferred_element_type=jnp.float32,
        )

    final = soil_ref.shape[0] - 1
    for b in range(rows):
        at = slice(b * width, (b + 1) * width)
        top_ref[b : b + 1, :] = soil_ref[0:1, at]
        deep_ref[b : b + 1, :] = soil_ref[final : final + 1, at]
        drain_ref[b : b + 1, :] = coef_ref[final : final + 1, at]
    top, deep = top_ref[...], deep_ref[...]
    runoff = rain_ref[...] * top * top + drain_ref[...] * deep * deep * deep
    share = runoff / SUB
    rate = rate_ref[...]
    storage = storage_ref[...]
    leaving = jnp.where(down == width, rate, 0.0)
    powers = [leaving]
    for _ in range(SUB - 1):
        powers.append(powers[-1] * leaving)
    sums = jnp.zeros((rows, width), jnp.float32)
    column = 0
    for power in powers:
        sums = sums + product(power * storage, ones_where(second == column))
        column += 1
    for turn in range(SUB):
        release = rate * storage
        upto = pick(product(pick(release, order), before), ends)
        upstream = jnp.where(lane == 0, 0.0, upto - pltpu.roll(upto, 1, 1))
        gained = share + upstream
        up_ref[turn] = gained
        storage = storage + gained - release
        for power in powers[: SUB - 1 - turn]:
            sums = sums + product(power * gained, ones_where(second == column))
            column += 1
    moment_ref[pl.ds(pl.multiple_of(step * rows, rows), rows), :] = sums

    @pl.when(step == pl.num_programs(0) - 1)
    def _():
        flat = moment_ref[...].T[:16]
        mine = lax.broadcasted_iota(jnp.int32, (devices, blocks), 0) == owner_ref[...]
        mine = mine.astype(jnp.float32)[:, None, :]
        hits = lax.broadcasted_iota(jnp.int32, (reaches, blocks), 0) == reach_ref[...]
        hits = hits.astype(jnp.float32).astype(jnp.bfloat16)
        total = jnp.zeros((devices * 16, reaches), jnp.float32)
        for part in split(flat):
            spread = (mine * part.astype(jnp.float32)[None]).reshape(devices * 16, blocks)
            total = total + lax.dot_general(
                spread.astype(jnp.bfloat16),
                hits,
                (((1,), (1,)), ((), ())),
                preferred_element_type=jnp.float32,
            )
        agg_ref[...] = total.reshape(devices, 16, reaches)[:, :MOMENTS, :]


def land_step(soil_water, rainfall, drain_coef):
    top_layer = soil_water[:1]
    soaked = rainfall - rainfall * top_layer * top_layer
    drained = drain_coef * soil_water * soil_water * soil_water
    inflow = jnp.concatenate([soaked, drained[:-1]], axis=0)
    return soil_water + inflow - drained


def exchange_kernel(
    groups,
    devices,
    agg_ref,
    volume_ref,
    lag_ref,
    soil_hbm,
    coef_hbm,
    rain_hbm,
    out_ref,
    mid_ref,
    soil_ref,
    coef_ref,
    rain_ref,
    load_sem,
    landed,
    mine,
    send_sem,
    recv_sem,
    send_all,
    recv_all,
):
    me = lax.axis_index("tile") * groups + lax.axis_index("grp")

    def peer_at(step):
        peer = lax.rem(me + step, devices)
        return peer, (peer // groups, lax.rem(peer, groups))

    loads = [
        pltpu.make_async_copy(soil_hbm, soil_ref, load_sem.at[0]),
        pltpu.make_async_copy(coef_hbm, coef_ref, load_sem.at[1]),
        pltpu.make_async_copy(rain_hbm, rain_ref, load_sem.at[2]),
    ]
    for load in loads:
        load.start()
    barrier = pltpu.get_barrier_semaphore()

    def greet(step, carry):
        pl.semaphore_signal(barrier, inc=1, device_id=peer_at(step)[1], device_id_type=MESH)
        return carry

    lax.fori_loop(1, devices, greet, 0)
    pl.semaphore_wait(barrier, devices - 1)

    def part(step):
        peer, place = peer_at(step)
        return pltpu.make_async_remote_copy(
            src_ref=agg_ref.at[peer],
            dst_ref=landed.at[step],
            send_sem=send_sem.at[step],
            recv_sem=recv_sem.at[step],
            device_id=place,
            device_id_type=MESH,
        )

    def whole(step):
        return pltpu.make_async_remote_copy(
            src_ref=mine,
            dst_ref=out_ref.at[me],
            send_sem=send_all.at[step],
            recv_sem=recv_all.at[step],
            device_id=peer_at(step)[1],
            device_id_type=MESH,
        )

    def start(copy):
        def body(step, carry):
            copy(step).start()
            return carry

        lax.fori_loop(1, devices, body, 0)

    def finish(copy):
        def body(step, carry):
            copy(step).wait()
            return carry

        lax.fori_loop(1, devices, body, 0)

    start(part)
    landed[0] = agg_ref[me]
    span = math.gcd(soil_ref.shape[1], 2048)

    def land(turn, carry):
        at = pl.ds(pl.multiple_of(turn * span, span), span)
        mid_ref[:, at] = land_step(soil_ref[:, at], rain_ref[:, at], coef_ref[:, at])
        return carry

    for load in loads:
        load.wait()
    lax.fori_loop(0, soil_ref.shape[1] // span, land, 0)
    finish(part)
    mine[pl.ds(0, MOMENTS), :] = jnp.sum(landed[...], axis=0)
    mine[pl.ds(MOMENTS, 1), :] = volume_ref[...]
    mine[pl.ds(MOMENTS + 1, 1), :] = lag_ref[...]
    start(whole)
    out_ref[me] = mine[...]
    finish(whole)


def simulate(groups, river, width):
    devices, reaches = river[0].shape
    shape = (devices, reaches)
    lane = lanes_of(shape)
    row = lax.broadcasted_iota(jnp.int32, shape, 0)
    volume, lag = river[MOMENTS], river[MOMENTS + 1]
    weight = 1.0 / (1.0 + lag)
    held = list(river[:SUB])
    gained, at = [], SUB
    for turn in range(SUB - 1):
        gained.append(river[at : at + SUB - 1 - turn])
        at += SUB - 1 - turn

    def ladder(gain, place, axis, first, size):
        steps, step = [], first
        while step < size:
            inside = place >= step
            steps.append((step, jnp.where(inside, gain, 0.0)))
            gain = jnp.where(inside, gain * pltpu.roll(gain, step, axis), gain)
            step *= 2
        return steps, gain

    def climb(steps, value, axis):
        for step, gain in steps:
            value = value + gain * pltpu.roll(value, step, axis)
        return value

    def last(value):
        return jnp.broadcast_to(value[:, reaches - 1 :], shape)

    within, gain = ladder(weight, lane, 1, 1, reaches)
    across, _ = ladder(last(gain), row, 0, groups, devices)
    backs, flow = [], volume
    for turn in range(SUB):
        back = 1.0 / (1.0 + volume)
        backs.append(back)
        feed = weight * (volume + back * held[0] / width)
        offset = climb(within, feed, 1)
        head = climb(across, last(offset), 0)
        if devices > groups:
            head = jnp.where(row >= groups, pltpu.roll(head, groups, 0), 0.0)
        else:
            head = jnp.zeros_like(head)
        flow = gain * head + offset
        volume = lag * flow
        if turn < SUB - 1:
            held = [
                held[j] + gained[turn][j] - back * held[j + 1] for j in range(SUB - 1 - turn)
            ]
    return backs, flow


def settle_kernel(
    groups,
    river_ref,
    storage_ref,
    rate_ref,
    down_ref,
    owner_ref,
    reach_ref,
    up_ref,
    mid_ref,
    storage_out_ref,
    section_ref,
    soil_out_ref,
    table_ref,
    place_ref,
    wet_ref,
):
    step = pl.program_id(0)
    rows, width = storage_ref.shape
    devices, _, reaches = river_ref.shape
    blocks = owner_ref.shape[1]

    @pl.when(step == 0)
    def _():
        river = [river_ref[:, m, :] for m in range(MOMENTS + 2)]
        backs, flow = simulate(groups, river, width)
        me = lax.axis_index("tile") * groups + lax.axis_index("grp")
        own = lax.broadcasted_iota(jnp.int32, flow.shape, 0) == me
        section_ref[...] = jnp.log1p(jnp.sum(jnp.where(own, flow, 0.0), axis=0, keepdims=True))
        for turn in range(SUB):
            high, low = split(backs[turn])
            table_ref[0, :, turn * reaches : (turn + 1) * reaches] = high
            table_ref[1, :, turn * reaches : (turn + 1) * reaches] = low
        both = jnp.concatenate(
            [
                jnp.broadcast_to(owner_ref[...].astype(jnp.float32), (8, blocks)),
                jnp.broadcast_to(reach_ref[...].astype(jnp.float32), (8, blocks)),
                jnp.zeros((112, blocks), jnp.float32),
            ],
            axis=0,
        )
        place_ref[...] = both.T

    place = place_ref[pl.ds(pl.multiple_of(step * rows, rows), rows), :].astype(jnp.int32)
    owner, reach = place[:, 0:1], place[:, 8:9]
    mine = (lanes_of((rows, devices)) == owner).astype(jnp.float32).astype(jnp.bfloat16)
    found = jnp.dot(mine, table_ref[0], preferred_element_type=jnp.float32) + jnp.dot(
        mine, table_ref[1], preferred_element_type=jnp.float32
    )
    hit = lanes_of((rows, reaches)) == reach
    leaving = down_ref[...] == width
    rate = rate_ref[...]
    storage = storage_ref[...]
    for turn in range(SUB):
        back = jnp.sum(
            jnp.where(hit, found[:, turn * reaches : (turn + 1) * reaches], 0.0),
            axis=1,
            keepdims=True,
        )
        release = rate * storage * jnp.where(leaving, back, 1.0)
        storage = storage + up_ref[turn] - release
    storage_out_ref[...] = storage
    wet_ref[...] = recharge_share * (storage / (storage + 1.0))
    soil_out_ref[1:, :] = mid_ref[1:, :]
    for b in range(rows):
        at = slice(b * width, (b + 1) * width)
        top = mid_ref[0:1, at]
        soil_out_ref[0:1, at] = top + wet_ref[b : b + 1, :] * (1.0 - top)


def local(
    soil_water,
    rainfall,
    drain_coef,
    cell_storage,
    release_rate,
    downstream,
    block_owner,
    outlet_reach,
    river_storage,
    river_lag,
):
    groups = lax.axis_size("grp")
    devices = lax.axis_size("tile") * groups
    blocks = block_owner.shape[0]
    width = rainfall.shape[0] // blocks
    reaches = river_storage.shape[1]
    rows = math.gcd(blocks, 128)
    rain = rainfall.reshape(blocks, width)
    storage = cell_storage.reshape(blocks, width)
    rate = release_rate.reshape(blocks, width)
    down = downstream.reshape(blocks, width)
    owner = block_owner.reshape(1, blocks)
    reach = outlet_reach.reshape(1, blocks)

    tile = pl.BlockSpec((rows, width), lambda i: (i, 0))
    layers = soil_water.shape[0]
    slab = pl.BlockSpec((layers, rows * width), lambda i: (0, i))
    line = pl.BlockSpec((1, blocks), lambda i: (0, 0))
    stack = pl.BlockSpec((SUB, rows, width), lambda i: (0, i, 0))
    gained, agg = pl.pallas_call(
        route_kernel,
        grid=(blocks // rows,),
        out_shape=(
            jax.ShapeDtypeStruct((SUB, blocks, width), jnp.float32),
            jax.ShapeDtypeStruct((devices, MOMENTS, reaches), jnp.float32),
        ),
        in_specs=[slab, slab, tile, tile, tile, tile, line, line],
        out_specs=(stack, pl.BlockSpec((devices, MOMENTS, reaches), lambda i: (0, 0, 0))),
        scratch_shapes=[pltpu.VMEM((blocks, width), jnp.float32)]
        + [pltpu.VMEM((rows, width), jnp.float32)] * 3,
        compiler_params=pltpu.CompilerParams(vmem_limit_bytes=63 * 1024 * 1024),
    )(soil_water, drain_coef, rain, storage, rate, down, owner, reach)

    vmem = pl.BlockSpec(memory_space=pltpu.VMEM)
    river, soil_mid = pl.pallas_call(
        functools.partial(exchange_kernel, groups, devices),
        out_shape=(
            jax.ShapeDtypeStruct((devices, MOMENTS + 2, reaches), jnp.float32),
            jax.ShapeDtypeStruct(soil_water.shape, jnp.float32),
        ),
        in_specs=[vmem] * 3 + [pl.BlockSpec(memory_space=pl.ANY)] * 3,
        out_specs=(vmem, vmem),
        scratch_shapes=[
            pltpu.VMEM(soil_water.shape, jnp.float32),
            pltpu.VMEM(soil_water.shape, jnp.float32),
            pltpu.VMEM((1, soil_water.shape[1]), jnp.float32),
            pltpu.SemaphoreType.DMA((3,)),
            pltpu.VMEM((devices, MOMENTS, reaches), jnp.float32),
            pltpu.VMEM((MOMENTS + 2, reaches), jnp.float32),
            pltpu.SemaphoreType.DMA((devices,)),
            pltpu.SemaphoreType.DMA((devices,)),
            pltpu.SemaphoreType.DMA((devices,)),
            pltpu.SemaphoreType.DMA((devices,)),
        ],
        compiler_params=pltpu.CompilerParams(
            collective_id=0, has_side_effects=True, vmem_limit_bytes=63 * 1024 * 1024
        ),
    )(agg, river_storage, river_lag, soil_water, drain_coef, rainfall[None])

    storage_out, section, soil_out = pl.pallas_call(
        functools.partial(settle_kernel, groups),
        grid=(blocks // rows,),
        out_shape=(
            jax.ShapeDtypeStruct((blocks, width), jnp.float32),
            jax.ShapeDtypeStruct((1, reaches), jnp.float32),
            jax.ShapeDtypeStruct(soil_water.shape, jnp.float32),
        ),
        in_specs=[
            pl.BlockSpec((devices, MOMENTS + 2, reaches), lambda i: (0, 0, 0)),
            tile,
            tile,
            tile,
            line,
            line,
            stack,
            slab,
        ],
        out_specs=(tile, pl.BlockSpec((1, reaches), lambda i: (0, 0)), slab),
        scratch_shapes=[
            pltpu.VMEM((2, devices, SUB * reaches), jnp.bfloat16),
            pltpu.VMEM((blocks, 128), jnp.float32),
            pltpu.VMEM((rows, width), jnp.float32),
        ],
        compiler_params=pltpu.CompilerParams(vmem_limit_bytes=63 * 1024 * 1024),
    )(river, storage, rate, down, owner, reach, gained, soil_mid)

    return (soil_out, storage_out.reshape(-1), section)


def solution(mesh):
    placed = (
        P(None, ("tile", "grp")),
        P(("tile", "grp")),
        P(None, ("tile", "grp")),
        P(("tile", "grp")),
        P(("tile", "grp")),
        P(("tile", "grp")),
        P(("tile", "grp"), None),
        P(("tile", "grp")),
        P("grp", "tile"),
        P("grp", "tile"),
    )
    return jax.shard_map(
        local,
        mesh=mesh,
        in_specs=placed,
        out_specs=(P(None, ("tile", "grp")), P(("tile", "grp")), P("grp", "tile")),
        check_vma=False,
    )
```

```python
import functools
import math

import jax
import jax.numpy as jnp
from jax import lax
from jax.experimental import pallas as pl
from jax.experimental.pallas import tpu as pltpu
from jax.sharding import PartitionSpec as P

SUB = 4
MOMENTS = SUB * (SUB + 1) // 2
MESH = pl.DeviceIdType.MESH

recharge_share = 0.2


def split(x):
    high = x.astype(jnp.bfloat16)
    low = (x - high.astype(jnp.float32)).astype(jnp.bfloat16)
    return high, low


def lanes_of(shape):
    return lax.broadcasted_iota(jnp.int32, shape, len(shape) - 1)


def ones_where(mask):
    return mask.astype(jnp.float32).astype(jnp.bfloat16)


def pick(values, index):
    return jnp.take_along_axis(values, index, axis=1)


def sort_rows(key):
    width = key.shape[1]
    count = width // 8
    flipped = key.T
    parts = [flipped[v * 8 : v * 8 + 8] for v in range(count)]
    line = lax.broadcasted_iota(jnp.int32, parts[0].shape, 0)
    size = 2
    while size <= width:
        step = size // 2
        while step:
            after = list(parts)
            if step < count:
                for v in range(count):
                    if v & step:
                        continue
                    small = jnp.minimum(parts[v], parts[v | step])
                    large = jnp.maximum(parts[v], parts[v | step])
                    if size < count:
                        falling = bool(v & size)
                        after[v], after[v | step] = (large, small) if falling else (small, large)
                    elif size == width:
                        after[v], after[v | step] = small, large
                    else:
                        falling = (line & (size // count)) != 0
                        after[v] = jnp.where(falling, large, small)
                        after[v | step] = jnp.where(falling, small, large)
            else:
                hop = step // count
                upper = (line & hop) != 0
                low = jnp.logical_xor(upper, (line & (size // count)) == 0)
                for v in range(count):
                    here = parts[v]
                    other = jnp.where(upper, pltpu.roll(here, hop, 0), pltpu.roll(here, 8 - hop, 0))
                    after[v] = jnp.where(low, jnp.minimum(here, other), jnp.maximum(here, other))
            parts = after
            step //= 2
        size *= 2
    rows = jnp.concatenate(parts, axis=0).T
    lane = lanes_of(rows.shape)
    return pick(rows, (lane % count) * 8 + lane // count)


def route_kernel(
    soil_ref,
    coef_ref,
    rain_ref,
    storage_ref,
    rate_ref,
    down_ref,
    owner_ref,
    reach_ref,
    up_ref,
    agg_ref,
    moment_ref,
    top_ref,
    deep_ref,
    drain_ref,
):
    step = pl.program_id(0)
    rows, width = storage_ref.shape
    devices, _, reaches = agg_ref.shape
    blocks = owner_ref.shape[1]
    lane = lanes_of((rows, width))
    down = down_ref[...]
    key = sort_rows((down * width + lane).astype(jnp.float32)).astype(jnp.int32)
    order = key % width
    target = key // width
    ends = jnp.zeros_like(lane)
    hop = width // 2
    while hop:
        ends = jnp.where(pick(target, ends + (hop - 1)) <= lane, ends + hop, ends)
        hop //= 2
    square = (width, width)
    first, second = lax.broadcasted_iota(jnp.int32, square, 0), lanes_of(square)
    before = ones_where(first < second)

    def product(value, ones):
        return jnp.dot(
            jnp.concatenate(split(value), axis=1),
            jnp.concatenate([ones, ones], axis=0),
            preferred_element_type=jnp.float32,
        )

    final = soil_ref.shape[0] - 1
    for b in range(rows):
        at = slice(b * width, (b + 1) * width)
        top_ref[b : b + 1, :] = soil_ref[0:1, at]
        deep_ref[b : b + 1, :] = soil_ref[final : final + 1, at]
        drain_ref[b : b + 1, :] = coef_ref[final : final + 1, at]
    top, deep = top_ref[...], deep_ref[...]
    runoff = rain_ref[...] * top * top + drain_ref[...] * deep * deep * deep
    share = runoff / SUB
    rate = rate_ref[...]
    storage = storage_ref[...]
    leaving = jnp.where(down == width, rate, 0.0)
    powers = [leaving]
    for _ in range(SUB - 1):
        powers.append(powers[-1] * leaving)
    sums = jnp.zeros((rows, width), jnp.float32)
    column = 0
    for power in powers:
        sums = sums + product(power * storage, ones_where(second == column))
        column += 1
    for turn in range(SUB):
        release = rate * storage
        upto = pick(product(pick(release, order), before), ends)
        upstream = jnp.where(lane == 0, 0.0, upto - pltpu.roll(upto, 1, 1))
        gained = share + upstream
        up_ref[turn] = gained
        storage = storage + gained - release
        for power in powers[: SUB - 1 - turn]:
            sums = sums + product(power * gained, ones_where(second == column))
            column += 1
    moment_ref[pl.ds(pl.multiple_of(step * rows, rows), rows), :] = sums

    @pl.when(step == pl.num_programs(0) - 1)
    def _():
        flat = moment_ref[...].T[:16]
        mine = lax.broadcasted_iota(jnp.int32, (devices, blocks), 0) == owner_ref[...]
        mine = mine.astype(jnp.float32)[:, None, :]
        hits = lax.broadcasted_iota(jnp.int32, (reaches, blocks), 0) == reach_ref[...]
        hits = hits.astype(jnp.float32).astype(jnp.bfloat16)
        total = jnp.zeros((devices * 16, reaches), jnp.float32)
        for part in split(flat):
            spread = (mine * part.astype(jnp.float32)[None]).reshape(devices * 16, blocks)
            total = total + lax.dot_general(
                spread.astype(jnp.bfloat16),
                hits,
                (((1,), (1,)), ((), ())),
                preferred_element_type=jnp.float32,
            )
        agg_ref[...] = total.reshape(devices, 16, reaches)[:, :MOMENTS, :]


def land_step(soil_water, rainfall, drain_coef):
    top_layer = soil_water[:1]
    soaked = rainfall - rainfall * top_layer * top_layer
    drained = drain_coef * soil_water * soil_water * soil_water
    inflow = jnp.concatenate([soaked, drained[:-1]], axis=0)
    return soil_water + inflow - drained


def exchange_kernel(
    groups,
    devices,
    agg_ref,
    volume_ref,
    lag_ref,
    soil_hbm,
    coef_hbm,
    rain_hbm,
    out_ref,
    mid_hbm,
    mid_ref,
    soil_ref,
    coef_ref,
    rain_ref,
    load_sem,
    landed,
    mine,
    send_sem,
    recv_sem,
    send_all,
    recv_all,
):
    me = lax.axis_index("tile") * groups + lax.axis_index("grp")

    def peer_at(step):
        peer = lax.rem(me + step, devices)
        return peer, (peer // groups, lax.rem(peer, groups))

    loads = [
        pltpu.make_async_copy(soil_hbm, soil_ref, load_sem.at[0]),
        pltpu.make_async_copy(coef_hbm, coef_ref, load_sem.at[1]),
        pltpu.make_async_copy(rain_hbm, rain_ref, load_sem.at[2]),
    ]
    for load in loads:
        load.start()
    barrier = pltpu.get_barrier_semaphore()

    def greet(step, carry):
        pl.semaphore_signal(barrier, inc=1, device_id=peer_at(step)[1], device_id_type=MESH)
        return carry

    lax.fori_loop(1, devices, greet, 0)
    pl.semaphore_wait(barrier, devices - 1)

    def part(step):
        peer, place = peer_at(step)
        return pltpu.make_async_remote_copy(
            src_ref=agg_ref.at[peer],
            dst_ref=landed.at[step],
            send_sem=send_sem.at[step],
            recv_sem=recv_sem.at[step],
            device_id=place,
            device_id_type=MESH,
        )

    def whole(step):
        return pltpu.make_async_remote_copy(
            src_ref=mine,
            dst_ref=out_ref.at[me],
            send_sem=send_all.at[step],
            recv_sem=recv_all.at[step],
            device_id=peer_at(step)[1],
            device_id_type=MESH,
        )

    def start(copy):
        def body(step, carry):
            copy(step).start()
            return carry

        lax.fori_loop(1, devices, body, 0)

    def finish(copy):
        def body(step, carry):
            copy(step).wait()
            return carry

        lax.fori_loop(1, devices, body, 0)

    start(part)
    landed[0] = agg_ref[me]
    span = math.gcd(soil_ref.shape[1], 2048)

    def land(turn, carry):
        at = pl.ds(pl.multiple_of(turn * span, span), span)
        mid_ref[:, at] = land_step(soil_ref[:, at], rain_ref[:, at], coef_ref[:, at])
        return carry

    for load in loads:
        load.wait()
    lax.fori_loop(0, soil_ref.shape[1] // span, land, 0)
    store = pltpu.make_async_copy(mid_ref, mid_hbm, load_sem.at[3])
    store.start()
    finish(part)
    mine[pl.ds(0, MOMENTS), :] = jnp.sum(landed[...], axis=0)
    mine[pl.ds(MOMENTS, 1), :] = volume_ref[...]
    mine[pl.ds(MOMENTS + 1, 1), :] = lag_ref[...]
    start(whole)
    out_ref[me] = mine[...]
    finish(whole)
    store.wait()


def simulate(groups, river, width):
    devices, reaches = river[0].shape
    shape = (devices, reaches)
    lane = lanes_of(shape)
    row = lax.broadcasted_iota(jnp.int32, shape, 0)
    volume, lag = river[MOMENTS], river[MOMENTS + 1]
    weight = 1.0 / (1.0 + lag)
    held = list(river[:SUB])
    gained, at = [], SUB
    for turn in range(SUB - 1):
        gained.append(river[at : at + SUB - 1 - turn])
        at += SUB - 1 - turn

    def ladder(gain, place, axis, first, size):
        steps, step = [], first
        while step < size:
            inside = place >= step
            steps.append((step, jnp.where(inside, gain, 0.0)))
            gain = jnp.where(inside, gain * pltpu.roll(gain, step, axis), gain)
            step *= 2
        return steps, gain

    def climb(steps, value, axis):
        for step, gain in steps:
            value = value + gain * pltpu.roll(value, step, axis)
        return value

    def last(value):
        return jnp.broadcast_to(value[:, reaches - 1 :], shape)

    within, gain = ladder(weight, lane, 1, 1, reaches)
    across, _ = ladder(last(gain), row, 0, groups, devices)
    backs, flow = [], volume
    for turn in range(SUB):
        back = 1.0 / (1.0 + volume)
        backs.append(back)
        feed = weight * (volume + back * held[0] / width)
        offset = climb(within, feed, 1)
        head = climb(across, last(offset), 0)
        if devices > groups:
            head = jnp.where(row >= groups, pltpu.roll(head, groups, 0), 0.0)
        else:
            head = jnp.zeros_like(head)
        flow = gain * head + offset
        volume = lag * flow
        if turn < SUB - 1:
            held = [
                held[j] + gained[turn][j] - back * held[j + 1] for j in range(SUB - 1 - turn)
            ]
    return backs, flow


def settle_kernel(
    groups,
    river_ref,
    storage_ref,
    rate_ref,
    down_ref,
    owner_ref,
    reach_ref,
    up_ref,
    mid_ref,
    storage_out_ref,
    section_ref,
    soil_out_ref,
    table_ref,
    place_ref,
    wet_ref,
):
    step = pl.program_id(0)
    rows, width = storage_ref.shape
    devices, _, reaches = river_ref.shape
    blocks = owner_ref.shape[1]

    @pl.when(step == 0)
    def _():
        river = [river_ref[:, m, :] for m in range(MOMENTS + 2)]
        backs, flow = simulate(groups, river, width)
        me = lax.axis_index("tile") * groups + lax.axis_index("grp")
        own = lax.broadcasted_iota(jnp.int32, flow.shape, 0) == me
        section_ref[...] = jnp.log1p(jnp.sum(jnp.where(own, flow, 0.0), axis=0, keepdims=True))
        for turn in range(SUB):
            high, low = split(backs[turn])
            table_ref[0, :, turn * reaches : (turn + 1) * reaches] = high
            table_ref[1, :, turn * reaches : (turn + 1) * reaches] = low
        both = jnp.concatenate(
            [
                jnp.broadcast_to(owner_ref[...].astype(jnp.float32), (8, blocks)),
                jnp.broadcast_to(reach_ref[...].astype(jnp.float32), (8, blocks)),
                jnp.zeros((112, blocks), jnp.float32),
            ],
            axis=0,
        )
        place_ref[...] = both.T

    place = place_ref[pl.ds(pl.multiple_of(step * rows, rows), rows), :].astype(jnp.int32)
    owner, reach = place[:, 0:1], place[:, 8:9]
    mine = (lanes_of((rows, devices)) == owner).astype(jnp.float32).astype(jnp.bfloat16)
    found = jnp.dot(mine, table_ref[0], preferred_element_type=jnp.float32) + jnp.dot(
        mine, table_ref[1], preferred_element_type=jnp.float32
    )
    hit = lanes_of((rows, reaches)) == reach
    leaving = down_ref[...] == width
    rate = rate_ref[...]
    storage = storage_ref[...]
    for turn in range(SUB):
        back = jnp.sum(
            jnp.where(hit, found[:, turn * reaches : (turn + 1) * reaches], 0.0),
            axis=1,
            keepdims=True,
        )
        release = rate * storage * jnp.where(leaving, back, 1.0)
        storage = storage + up_ref[turn] - release
    storage_out_ref[...] = storage
    wet_ref[...] = recharge_share * (storage / (storage + 1.0))
    soil_out_ref[1:, :] = mid_ref[1:, :]
    for b in range(rows):
        at = slice(b * width, (b + 1) * width)
        top = mid_ref[0:1, at]
        soil_out_ref[0:1, at] = top + wet_ref[b : b + 1, :] * (1.0 - top)


def local(
    soil_water,
    rainfall,
    drain_coef,
    cell_storage,
    release_rate,
    downstream,
    block_owner,
    outlet_reach,
    river_storage,
    river_lag,
):
    groups = lax.axis_size("grp")
    devices = lax.axis_size("tile") * groups
    blocks = block_owner.shape[0]
    width = rainfall.shape[0] // blocks
    reaches = river_storage.shape[1]
    rows = math.gcd(blocks, 128)
    rain = rainfall.reshape(blocks, width)
    storage = cell_storage.reshape(blocks, width)
    rate = release_rate.reshape(blocks, width)
    down = downstream.reshape(blocks, width)
    owner = block_owner.reshape(1, blocks)
    reach = outlet_reach.reshape(1, blocks)

    tile = pl.BlockSpec((rows, width), lambda i: (i, 0))
    layers = soil_water.shape[0]
    slab = pl.BlockSpec((layers, rows * width), lambda i: (0, i))
    line = pl.BlockSpec((1, blocks), lambda i: (0, 0))
    stack = pl.BlockSpec((SUB, rows, width), lambda i: (0, i, 0))
    gained, agg = pl.pallas_call(
        route_kernel,
        grid=(blocks // rows,),
        out_shape=(
            jax.ShapeDtypeStruct((SUB, blocks, width), jnp.float32),
            jax.ShapeDtypeStruct((devices, MOMENTS, reaches), jnp.float32),
        ),
        in_specs=[slab, slab, tile, tile, tile, tile, line, line],
        out_specs=(stack, pl.BlockSpec((devices, MOMENTS, reaches), lambda i: (0, 0, 0))),
        scratch_shapes=[pltpu.VMEM((blocks, width), jnp.float32)]
        + [pltpu.VMEM((rows, width), jnp.float32)] * 3,
        compiler_params=pltpu.CompilerParams(vmem_limit_bytes=63 * 1024 * 1024),
    )(soil_water, drain_coef, rain, storage, rate, down, owner, reach)

    vmem = pl.BlockSpec(memory_space=pltpu.VMEM)
    river, soil_mid = pl.pallas_call(
        functools.partial(exchange_kernel, groups, devices),
        out_shape=(
            jax.ShapeDtypeStruct((devices, MOMENTS + 2, reaches), jnp.float32),
            jax.ShapeDtypeStruct(soil_water.shape, jnp.float32),
        ),
        in_specs=[vmem] * 3 + [pl.BlockSpec(memory_space=pl.ANY)] * 3,
        out_specs=(vmem, pl.BlockSpec(memory_space=pl.ANY)),
        scratch_shapes=[
            pltpu.VMEM(soil_water.shape, jnp.float32),
            pltpu.VMEM(soil_water.shape, jnp.float32),
            pltpu.VMEM(soil_water.shape, jnp.float32),
            pltpu.VMEM((1, soil_water.shape[1]), jnp.float32),
            pltpu.SemaphoreType.DMA((4,)),
            pltpu.VMEM((devices, MOMENTS, reaches), jnp.float32),
            pltpu.VMEM((MOMENTS + 2, reaches), jnp.float32),
            pltpu.SemaphoreType.DMA((devices,)),
            pltpu.SemaphoreType.DMA((devices,)),
            pltpu.SemaphoreType.DMA((devices,)),
            pltpu.SemaphoreType.DMA((devices,)),
        ],
        compiler_params=pltpu.CompilerParams(
            collective_id=0, has_side_effects=True, vmem_limit_bytes=63 * 1024 * 1024
        ),
    )(agg, river_storage, river_lag, soil_water, drain_coef, rainfall[None])

    storage_out, section, soil_out = pl.pallas_call(
        functools.partial(settle_kernel, groups),
        grid=(blocks // rows,),
        out_shape=(
            jax.ShapeDtypeStruct((blocks, width), jnp.float32),
            jax.ShapeDtypeStruct((1, reaches), jnp.float32),
            jax.ShapeDtypeStruct(soil_water.shape, jnp.float32),
        ),
        in_specs=[
            pl.BlockSpec((devices, MOMENTS + 2, reaches), lambda i: (0, 0, 0)),
            tile,
            tile,
            tile,
            line,
            line,
            stack,
            slab,
        ],
        out_specs=(tile, pl.BlockSpec((1, reaches), lambda i: (0, 0)), slab),
        scratch_shapes=[
            pltpu.VMEM((2, devices, SUB * reaches), jnp.bfloat16),
            pltpu.VMEM((blocks, 128), jnp.float32),
            pltpu.VMEM((rows, width), jnp.float32),
        ],
        compiler_params=pltpu.CompilerParams(vmem_limit_bytes=63 * 1024 * 1024),
    )(river, storage, rate, down, owner, reach, gained, soil_mid)

    return (soil_out, storage_out.reshape(-1), section)


def solution(mesh):
    placed = (
        P(None, ("tile", "grp")),
        P(("tile", "grp")),
        P(None, ("tile", "grp")),
        P(("tile", "grp")),
        P(("tile", "grp")),
        P(("tile", "grp")),
        P(("tile", "grp"), None),
        P(("tile", "grp")),
        P("grp", "tile"),
        P("grp", "tile"),
    )
    return jax.shard_map(
        local,
        mesh=mesh,
        in_specs=placed,
        out_specs=(P(None, ("tile", "grp")), P(("tile", "grp")), P("grp", "tile")),
        check_vma=False,
    )
```
